32 devices in a mesh: prow: 8 (over y, x, core), pcol: 4 (over z).
Axes of the slice: x: 2, y: 2, z: 4, core: 2. Of those that a mesh axis runs over, the one named last changes fastest.
Arguments:
- matrix: bfloat16 [4, 2048, 4, 1024], P(None, 'prow', None, 'pcol'), may hold values from -6 to 6
- pivots: int32 [2, 256], replicated, may hold values from 0 to 8191, as said below
- lower_inverse: bfloat16 [2, 256, 256], replicated, as said below
- upper_inverse: bfloat16 [2, 256, 256], replicated, as said below
Outputs:
- factored: bfloat16 [4, 2048, 4, 1024], P(None, 'prow', None, 'pcol')
The draws below stay inside these ranges and needn't reach their ends.
Inputs may be any that keep to these rules, and one draw needn't show every extreme that they name: For each panel k and each i, pivots[k, i] is either k * 256 + i or a row at or after (k + 1) * 256; entry 0 of each list is k * 256; the rows of one panel's list are distinct, and each list names row 8191. Each lower_inverse[k] is unit lower triangular. Each upper_inverse[k] is upper triangular with positive diagonal.
All inputs are finite; a program needn't handle non-finite values.
Results may differ from the reference program's by a relative error of at most 0.0079.
Values may be sent and summed in bfloat16 or wider, within the bound.
No kernel may reach another device: no remote copies, remote signals or barrier semaphores. Data moves between devices by JAX's collectives and lax.ppermute only.
A program may use at most 64 MiB of HBM per device.

```python
import jax
import jax.numpy as jnp
from jax import lax

NB = 256
RB = 4
CB = 4
PANELS = 2
ROWS = 8192
COLS = 4096
N_PROW = 8
N_PCOL = 4


def pivot_lists(key):
    lists = []
    for panel in range(PANELS):
        offset = panel * NB
        below_count = ROWS - offset - NB
        subkey = jax.random.fold_in(key, panel)
        candidate = jax.random.permutation(jax.random.fold_in(subkey, 1), below_count - 1)[:NB] + offset + NB
        place_at = jax.random.randint(jax.random.fold_in(subkey, 2), (), 1, NB)
        candidate = candidate.at[place_at].set(ROWS - 1)
        positions = jnp.arange(NB)
        unmoved = ((jax.random.randint(jax.random.fold_in(subkey, 3), (NB,), 0, 4) == 0) | (positions == 0)) & (positions != place_at)
        lists.append(jnp.where(unmoved, offset + positions, candidate))
    return jnp.stack(lists).astype(jnp.int32)


def draw_pivots(key, part):
    return pivot_lists(key)


def draw_lower_inverse(key, part):
    entries = jax.random.normal(key, (PANELS, NB, NB), jnp.float32)
    entries = entries * (0.5 / NB ** 0.5)
    result = jnp.tril(entries, -1) + jnp.eye(NB, dtype=jnp.float32)[None]
    return result.astype(jnp.bfloat16)


def draw_upper_inverse(key, part):
    first = jax.random.fold_in(key, 11)
    second = jax.random.fold_in(key, 12)
    entries = jax.random.normal(first, (PANELS, NB, NB), jnp.float32)
    diagonal = jax.random.uniform(second, (PANELS, NB), jnp.float32, 0.5, 1.5)
    entries = jnp.triu(entries * (0.5 / NB ** 0.5), 1)
    result = (entries + diagonal[:, :, None] * jnp.eye(NB, dtype=jnp.float32)[None]) * (1.0 / NB ** 0.5)
    return result.astype(jnp.bfloat16)


def block_scale(stream_key, shape, split, low, top_value):
    loudness = 1.0
    for dim, shards_of in split:
        draws = jax.random.uniform(jax.random.fold_in(jax.random.fold_in(stream_key, 6), dim), (shards_of,), jnp.float32, low / len(split), top_value / len(split))
        loudness = loudness * jnp.repeat(jnp.exp(draws), shape[dim] // shards_of).reshape((-1,) + (1,) * (len(shape) - 1 - dim))
    return loudness


def scatter_about(rng, shape, deviation, reach, cuts=(), kind=jnp.bfloat16):
    values = jax.random.normal(rng, shape, jnp.float32) * deviation
    if len(cuts) > 0:
        values = block_scale(rng, shape, cuts, -0.22, 0.18) * values
    return jnp.clip(values, min=-reach, max=reach).astype(kind)


def setup_inputs(seed: int = 0) -> dict:
    streams_of = jax.random.split(jax.random.key(seed), 5)
    return {
        "matrix": scatter_about(streams_of[0], (RB, N_PROW * NB, CB, N_PCOL * NB), 1.0, 6.0, ((1, 8), (3, 4))),
        "pivots": draw_pivots(jax.random.fold_in(streams_of[4], 71), 0),
        "lower_inverse": draw_lower_inverse(jax.random.fold_in(streams_of[4], 71), 0),
        "upper_inverse": draw_upper_inverse(jax.random.fold_in(streams_of[4], 71), 0),
    }


def reference(matrix, pivots, lower_inverse, upper_inverse):
    current = matrix.reshape(ROWS, COLS)
    row_index = jnp.arange(ROWS)
    col_index = jnp.arange(COLS)
    for panel in range(PANELS):
        start = panel * NB
        chosen = pivots[panel]
        old_top = current[start:start + NB]
        incoming = current[chosen]
        current = current.at[chosen].set(old_top)
        current = current.at[start:start + NB].set(incoming)
        lower = jnp.dot(current[:, start:start + NB], upper_inverse[panel], preferred_element_type=jnp.float32).astype(jnp.bfloat16)
        upper = jnp.dot(lower_inverse[panel], current[start:start + NB], preferred_element_type=jnp.float32).astype(jnp.bfloat16)
        row_mask = row_index >= start + NB
        col_mask = col_index >= start + NB

        def update_rows(item):
            block_rows, block_lower, block_mask = item
            product = jnp.dot(block_lower, upper, preferred_element_type=jnp.float32)
            changed = (block_rows.astype(jnp.float32) - product).astype(jnp.bfloat16)
            return jnp.where(block_mask[:, None] & col_mask[None, :], changed, block_rows)

        blocks = lax.map(update_rows, (current.reshape(ROWS // NB, NB, COLS), lower.reshape(ROWS // NB, NB, NB), row_mask.reshape(ROWS // NB, NB)))
        current = blocks.reshape(ROWS, COLS)
        current = current.at[start + NB:, start:start + NB].set(lower[start + NB:])
        current = current.at[start:start + NB, start + NB:].set(upper[:, start + NB:])
    return current.reshape(RB, N_PROW * NB, CB, N_PCOL * NB)
```

```python
import jax
import jax.numpy as jnp
from jax import lax
from jax.sharding import PartitionSpec as P


def levels_of(count):
    bits = count.bit_length() - 1
    return list(range(1, bits))


def exchange_pairs(count, level):
    order = levels_of(count)
    back = order[::-1]
    return [(i, i ^ (1 << (order[level] if i % 2 == 0 else back[level]))) for i in range(count)]


def spread_pairs(count, level):
    order = levels_of(count)
    back = order[::-1]
    pairs = []
    for parity, bits in ((0, order), (1, back)):
        held = [parity]
        for step in range(level):
            held += [i ^ (1 << bits[step]) for i in held]
        pairs += [(i, i ^ (1 << bits[level])) for i in held]
    return pairs


def far_steps(count):
    steps = []
    distance = count // 2
    while distance >= 2:
        steps.append([(i, i + distance) for i in range(count) if i % (2 * distance) < 2])
        distance //= 2
    return steps


def twin(count):
    return [(i, i ^ 1) for i in range(count)]


def member(index, targets):
    return sum((index == t).astype(jnp.int32) for t in targets) > 0


def local(matrix, pivots, lower_inverse, upper_inverse):
    nr = lax.axis_size("prow")
    nc = lax.axis_size("pcol")
    my_row = lax.axis_index("prow")
    my_col = lax.axis_index("pcol")
    down, block, across, _ = matrix.shape
    rows = down * block
    even_row = my_row % 2 == 0
    even_col = my_col % 2 == 0
    both = ("prow", "pcol")

    first, second = pivots[0], pivots[1]
    place = jnp.arange(block)
    hits = second[:, None] == first[None, :]
    second_source = jnp.where(hits.any(1), jnp.argmax(hits, 1), second)
    source = jnp.concatenate([first, second_source])
    after = jnp.where(first == place, place, first)
    moved = (first[:, None] == (block + place)[None, :])
    via_top = jnp.where(moved.any(1), jnp.sum(jnp.where(moved, second[None, :], 0), 1), after)
    back = first[:, None] == second[None, :]
    first_goes = jnp.where(back.any(1), block + jnp.argmax(back, 1), via_top)
    taken = (block + place)[:, None] == first[None, :]
    second_goes = jnp.where(taken.any(1), jnp.argmax(taken, 1), second)
    goes = jnp.concatenate([first_goes, second_goes])

    source_block = source // block
    mine = source_block % nr == my_row
    source_local = jnp.where(mine, source_block // nr * block + source % block, 0)
    flat = matrix.reshape(rows, across * block)
    picked = jnp.where(mine[:, None], flat[source_local], jnp.zeros((), jnp.bfloat16))

    own = matrix[:, :, 0, :]
    have, other = [], []
    for b in range(down):
        piece = own[b]
        for pairs in far_steps(nc):
            got = lax.ppermute(piece, "pcol", pairs)
            piece = jnp.where(member(my_col, [t for _, t in pairs]), got, piece)
        have.append(piece)
        other.append(lax.ppermute(piece, "pcol", twin(nc)))
    have = jnp.stack(have)
    other = jnp.stack(other)
    panel0 = jnp.where(even_col, have, other)
    panel1 = jnp.where(even_col, other, have)

    def gather_rows(part):
        keep = jnp.where(even_row, part[:block], part[block:])
        give = jnp.where(even_row, part[block:], part[:block])
        total = keep + lax.ppermute(give, "prow", twin(nr))
        for level in range(len(levels_of(nr))):
            total = total + lax.ppermute(total, "prow", exchange_pairs(nr, level))
        return total

    def pair_up(part):
        got = lax.ppermute(part, "prow", twin(nr))
        return jnp.where(even_row, part, got), jnp.where(even_row, got, part)

    head = gather_rows(picked[:, :block])
    tail = gather_rows(picked[:, block:])
    head0, head1 = pair_up(head)
    tail0, tail1 = pair_up(tail)
    rows0 = jnp.concatenate([head0, tail0], 1)
    rows1 = jnp.concatenate([head1, tail1], 1)

    side = head
    for pairs in far_steps(nc):
        joint = []
        for i in range(nr):
            joint += [(i * nc + s, i * nc + t) for s, t in pairs if s % 2 == (1 - i % 2)]
        got = lax.ppermute(side, both, joint)
        right = member(my_row * nc + my_col, [t for _, t in joint])
        side = jnp.where(right, got, side)
    joint = []
    for i in range(nr):
        joint += [(i * nc + s, i * nc + (s ^ 1)) for s in range(nc) if s % 2 == (1 - i % 2)]
    got = lax.ppermute(side, both, joint)
    side = jnp.where(member(my_row * nc + my_col, [t for _, t in joint]), got, side)
    side01, side10 = pair_up(side)

    def spread_rows(part):
        for level in range(len(levels_of(nr))):
            pairs = spread_pairs(nr, level)
            got = lax.ppermute(part, "prow", pairs)
            part = jnp.where(member(my_row, [t for _, t in pairs]), got, part)
        a, b = pair_up(part)
        return jnp.concatenate([a, b], 0)

    top = spread_rows(flat[:block])
    top_panels = spread_rows(jnp.concatenate([panel0[0], panel1[0]], 1))

    return finish(
        flat, rows0, rows1, side10, side01, top, top_panels, panel0, panel1,
        goes, lower_inverse, upper_inverse, my_row, my_col, nr, nc, matrix.shape,
    )


def finish(flat, rows0, rows1, side10, side01, top, top_panels, panel0, panel1,
           goes, lower_inverse, upper_inverse, my_row, my_col, nr, nc, shape):
    down, block, across, _ = shape
    f32, bf = jnp.float32, jnp.bfloat16
    dot = lambda a, b: jnp.dot(a, b, preferred_element_type=f32)
    u0 = dot(lower_inverse[0], rows0).astype(bf)
    u0p = dot(lower_inverse[0], side01).astype(bf)
    lp = dot(side10, upper_inverse[0]).astype(bf)
    r1 = (rows1.astype(f32) - dot(lp, u0)).astype(bf)
    u1 = dot(lower_inverse[1], r1).astype(bf)
    outs = []
    col = jnp.arange(across * block) // block * nc + my_col
    for b in range(down):
        g = (b * nr + my_row) * block + jnp.arange(block)
        onehot = (g[:, None] == goes[None, :]).astype(bf)
        hit = (g[:, None] == goes[None, :]).any(1)[:, None]
        s = jnp.where(hit, dot(onehot, top).astype(bf), flat[b * block:(b + 1) * block])
        tp = dot(onehot, top_panels).astype(bf)
        z0 = jnp.where(hit, tp[:, :block], panel0[b])
        z1 = jnp.where(hit, tp[:, block:], panel1[b])
        l0 = dot(z0, upper_inverse[0]).astype(bf)
        a1 = (s.astype(f32) - dot(l0, u0)).astype(bf)
        p1 = (z1.astype(f32) - dot(l0, u0p)).astype(bf)
        l1 = dot(p1, upper_inverse[1]).astype(bf)
        a2 = (a1.astype(f32) - dot(l1, u1)).astype(bf)
        wide = lambda x: jnp.tile(x, (1, across))
        body = jnp.where(col[None] == 0, wide(l0), jnp.where(col[None] == 1, wide(l1), a2))
        case0 = jnp.where(col[None] == 0, rows0, u0)
        case1 = jnp.where(col[None] == 0, wide(lp), jnp.where(col[None] == 1, r1, u1))
        gb = b * nr + my_row
        outs.append(jnp.where(gb == 0, case0, jnp.where(gb == 1, case1, body)))
    return jnp.concatenate(outs, 0).reshape(shape)


def solution(mesh):
    in_specs = (P(None, "prow", None, "pcol"), P(), P(), P())
    out_specs = P(None, "prow", None, "pcol")
    return jax.shard_map(local, mesh=mesh, in_specs=in_specs, out_specs=out_specs, check_vma=False)
```

```python
import functools

import jax
import jax.numpy as jnp
from jax import lax
from jax.experimental import pallas as pl
from jax.experimental.pallas import tpu as pltpu
from jax.sharding import PartitionSpec as P

BF, F32 = jnp.bfloat16, jnp.float32
VMEM = pl.BlockSpec(memory_space=pltpu.VMEM)
SMEM = pl.BlockSpec(memory_space=pltpu.SMEM)
ANY = pl.BlockSpec(memory_space=pl.ANY)
WEIGHT = 10**11


def bits_of(count):
    return list(range(1, count.bit_length() - 1))


def exchange_pairs(count, level):
    order = bits_of(count)
    return [(i, i ^ (1 << (order[level] if i % 2 == 0 else order[-1 - level]))) for i in range(count)]


def spread_pairs(count, levels):
    held, steps = [0, 1], []
    for level in levels:
        pairs = [pair for pair in exchange_pairs(count, level) if pair[0] in held]
        held = held + [target for _, target in pairs]
        steps.append(pairs)
    return steps


def far_steps(count):
    steps = []
    distance = count // 2
    while distance >= 2:
        steps.append([(i, i + distance) for i in range(count) if i % (2 * distance) < 2])
        distance //= 2
    return steps


def twin(count):
    return [(i, i ^ 1) for i in range(count)]


def member(index, pairs):
    return sum((index == t).astype(jnp.int32) for _, t in pairs) > 0


def after(value, *others):
    return lax.optimization_barrier((value, *others))[0]


def dot(a, b):
    return jnp.dot(a, b, preferred_element_type=F32)


def call(body, outs, args, in_specs, out_specs, scratch=(), flops=10**6):
    return pl.pallas_call(
        body,
        out_shape=outs,
        in_specs=in_specs,
        out_specs=out_specs,
        scratch_shapes=list(scratch),
        compiler_params=pltpu.CompilerParams(vmem_limit_bytes=24 << 20),
        cost_estimate=pl.CostEstimate(flops=flops, bytes_accessed=0, transcendentals=0),
    )(*args)


def first_kernel(a, piece, top, held, sem):
    copy = pltpu.make_async_copy(a.at[0], held, sem)
    copy.start()
    copy.wait()
    turned = jnp.transpose(held[...], (1, 0, 2))
    piece[...] = turned[0]
    top[...] = turned


def join_kernel(keep, got, top, out):
    across = keep.shape[0]
    out[:across] = keep[...] + got[...]
    out[across:] = top[...]


def merge_kernel(taken, part, got, out):
    across = part.shape[0] // 2
    out[:across] = part[:across] + got[:across]

    @pl.when(taken[0] > 0)
    def _():
        out[across:] = got[across:]

    @pl.when(taken[0] == 0)
    def _():
        out[across:] = part[across:]


def pick_kernel(nr, me, a, row, first_piece, flat, keep, give, middle, last, goes,
                raw, turned, hot, raw_sems, flat_sems):
    down, block, across, width = a.shape
    for b in range(down):
        pltpu.make_async_copy(a.at[b], raw.at[b], raw_sems.at[b]).start()
    my_row = me[0]
    even = my_row % 2 == 0
    first, second = row[0:1], row[1:2]
    i = lax.broadcasted_iota(jnp.int32, (block, block), 0)
    j = lax.broadcasted_iota(jnp.int32, (block, block), 1)

    def stand(line):
        line = jnp.where(i == j, line.astype(F32), 0.0)
        return jnp.sum(line, axis=1, keepdims=True).astype(jnp.int32)

    first_down, second_down = stand(first), stand(second)

    def found(mask, value, axis):
        value = jnp.where(mask, value.astype(F32), 0.0)
        count = jnp.sum(mask.astype(F32), axis=axis, keepdims=True)
        return count > 0.5, jnp.sum(value, axis=axis, keepdims=True).astype(jnp.int32)

    same = second_down == first
    hit, at = found(same, j, 1)
    second_source = jnp.where(hit, at, second_down)
    hit, at = found(first == block + i, jnp.broadcast_to(second_down, i.shape), 0)
    first_goes = jnp.where(hit, at, first)
    hit, at = found(same, i, 0)
    goes[0:1, :block] = jnp.where(hit, block + at, first_goes)
    hit, at = found(first_down == block + j, i, 0)
    goes[0:1, block:] = jnp.where(hit, at, second)

    kept = jnp.where(even, first_down, second_source)
    given = jnp.where(even, second_source, first_down)
    for b in range(down):
        base = (b * nr + my_row) * block
        hot[:block, b * block : (b + 1) * block] = (kept - base == j).astype(BF)
        hot[block:, b * block : (b + 1) * block] = (given - base == j).astype(BF)
    for b in range(down):
        pltpu.make_async_copy(a.at[b], raw.at[b], raw_sems.at[b]).wait()
        turned[:, b] = jnp.transpose(raw[b], (1, 0, 2))
        pltpu.make_async_copy(turned.at[:, b], flat.at[:, b], flat_sems.at[b]).start()
        if b == down - 1:
            last[...] = turned[0, b]
        elif b > 0:
            middle[b - 1] = turned[0, b]
    for c in range(across):
        picked = dot(hot[...], turned[c].reshape(down * block, width)).astype(BF)
        keep[c] = picked[:block]
        give[c] = picked[block:]
    for b in range(down):
        pltpu.make_async_copy(turned.at[:, b], flat.at[:, b], flat_sems.at[b]).wait()


def finish_kernel(nr, nc, parts, me, goes, lower, upper, *refs):
    across, down, block, width = refs[0].shape
    sources, rest = refs[:parts], refs[parts:]
    out = rest[0]
    held = rest[1 : 1 + parts]
    mix, u0, u1, r0, r1, result, in_sems, sems = rest[-8:]
    copies = [pltpu.make_async_copy(s, h, in_sems.at[k]) for k, (s, h) in enumerate(zip(sources, held))]
    for copy in copies:
        copy.start()
    flat, head_mine, head_other, tail_mine, tail_other, side_mine, side_other, top_mine, top_other = held[:9]
    rim_mine, rim_other = held[9:11]
    have, other = held[11:14], held[14:17]
    my_row, my_col = me[0], me[1]
    even = my_row % 2 == 0
    even_col = my_col % 2 == 0
    for k in range(1, 11):
        copies[k].wait()

    def both(mine, others):
        return jnp.where(even, mine, others), jnp.where(even, others, mine)

    side01, side10 = both(side_mine[...], side_other[...])
    u0p = dot(lower[0], side01).astype(BF)
    lp = dot(side10, upper[0]).astype(BF)
    for c in range(across):
        if c == 0:
            a0, a1 = both(head_mine[...], head_other[...])
        else:
            a0, a1 = both(tail_mine[c - 1], tail_other[c - 1])
        u = dot(lower[0], a0).astype(BF)
        a1 = (a1.astype(F32) - dot(lp, u)).astype(BF)
        if c == 0:
            r0[...] = a0
            r1[...] = a1
        t0, t1 = both(top_mine[c], top_other[c])
        mix[c, :block] = t0
        mix[c, block : 2 * block] = t1
        mix[c, 2 * block : 3 * block] = u
        mix[c, 3 * block :] = dot(lower[1], a1).astype(BF)
    rim = [jnp.concatenate(both(rim_mine[k], rim_other[k]), 0) for k in range(2)]
    for k in [0] + list(range(11, 17)):
        copies[k].wait()
    place = lax.broadcasted_iota(jnp.int32, (block, 2 * block), 0)
    for b in range(down):
        base = (b * nr + my_row) * block
        match = goes[...] - base == place
        onehot = match.astype(BF)
        hit = jnp.sum(match.astype(F32), axis=1, keepdims=True) > 0.5
        if b == 0:
            h, o = have[0][...], other[0][...]
        elif b == down - 1:
            h, o = have[2][...], other[2][...]
        else:
            h, o = have[1][b - 1], other[1][b - 1]
        z0 = jnp.where(hit, dot(onehot, rim[0]).astype(BF), jnp.where(even_col, h, o))
        z1 = jnp.where(hit, dot(onehot, rim[1]).astype(BF), jnp.where(even_col, o, h))
        l0 = dot(z0, upper[0]).astype(BF)
        l1 = dot((z1.astype(F32) - dot(l0, u0p)).astype(BF), upper[1]).astype(BF)
        factors = jnp.concatenate([onehot, -l0, -l1], 1)
        blocks = []
        for c in range(across):
            kept = jnp.where(hit, jnp.zeros((), BF), flat[c, b])
            s = (kept.astype(F32) + dot(factors, mix[c])).astype(BF)
            if c == 0:
                s = jnp.where(my_col == 0, l0, jnp.where(my_col == 1, l1, s))
            if b == 0:
                w0, w1 = mix[c, 2 * block : 3 * block], mix[c, 3 * block :]
                if c == 0:
                    w0 = jnp.where(my_col == 0, r0[...], w0)
                    w1 = jnp.where(my_col == 0, lp, jnp.where(my_col == 1, r1[...], w1))
                s = jnp.where(my_row == 0, w0, jnp.where(my_row == 1, w1, s))
            blocks.append(s)
        result[b] = jnp.transpose(jnp.stack(blocks), (1, 0, 2))
        pltpu.make_async_copy(result.at[b], out.at[b], sems.at[b]).start()
    for b in range(down):
        pltpu.make_async_copy(result.at[b], out.at[b], sems.at[b]).wait()


def local(matrix, pivots, lower_inverse, upper_inverse):
    nr = lax.axis_size("prow")
    nc = lax.axis_size("pcol")
    my_row = lax.axis_index("prow")
    my_col = lax.axis_index("pcol")
    down, block, across, width = matrix.shape
    joined = ("prow", "pcol")
    me = jnp.stack([my_row, my_col]).astype(jnp.int32)
    even_col = my_col % 2 == 0
    shape = lambda *s: jax.ShapeDtypeStruct(s, BF)
    depth = len(bits_of(nr))
    top_steps = spread_pairs(nr, [depth - 1] + list(range(depth - 1)) if depth else [])
    rim_steps = spread_pairs(nr, list(range(depth)))

    def far(piece):
        for pairs in far_steps(nc):
            got = lax.ppermute(piece, "pcol", pairs)
            piece = jnp.where(member(my_col, pairs), got, piece)
        return piece

    def near(piece):
        return lax.ppermute(piece, "pcol", twin(nc))

    def swap(part):
        return lax.ppermute(part, "prow", twin(nr))

    def pick(pairs, got, part):
        return jnp.where(member(my_row, pairs), got, part)

    first_piece, top = call(
        first_kernel, [shape(block, width), shape(across, block, width)], [matrix], [ANY], [VMEM] * 2,
        [pltpu.VMEM((block, across, width), BF), pltpu.SemaphoreType.DMA],
    )
    have0 = far(first_piece)
    for pairs in top_steps[:1]:
        top = pick(pairs, lax.ppermute(top, "prow", pairs), top)

    flat, keep, give, middle, last, goes = call(
        functools.partial(pick_kernel, nr),
        [shape(across, down, block, width), shape(across, block, width),
         shape(across, block, width), shape(down - 2, block, width), shape(block, width),
         jax.ShapeDtypeStruct((1, 2 * block), jnp.int32)],
        [me, matrix, pivots, first_piece],
        [SMEM, ANY, VMEM, ANY],
        [ANY] + [VMEM] * 5,
        [pltpu.VMEM(matrix.shape, BF), pltpu.VMEM((across, down, block, width), BF),
         pltpu.VMEM((2 * block, down * block), BF),
         pltpu.SemaphoreType.DMA((down,)), pltpu.SemaphoreType.DMA((down,))],
    )
    have1, have2 = far(middle), far(last)
    other0 = near(after(have0, keep))
    rim = jnp.stack([jnp.where(even_col, have0, other0), jnp.where(even_col, other0, have0)])

    part = call(
        join_kernel, shape(2 * across, block, width), [keep, swap(after(give, have0)), top], [VMEM] * 3, VMEM, flops=WEIGHT
    )
    for pairs in rim_steps[:-1]:
        rim = pick(pairs, lax.ppermute(after(rim, have1), "prow", pairs), rim)
    for level in range(depth - 1):
        pairs = exchange_pairs(nr, level)
        taken = member(my_row, top_steps[level + 1]).astype(jnp.int32)[None]
        part = call(
            merge_kernel, shape(2 * across, block, width), [taken, part, lax.ppermute(part, "prow", pairs)],
            [SMEM, VMEM, VMEM], VMEM, flops=WEIGHT,
        )
    head, tail, top = part[0], part[1:across], part[across:]
    if depth > 0:
        pairs = exchange_pairs(nr, depth - 1)
        head = head + lax.ppermute(head, "prow", pairs)
        got = lax.ppermute(jnp.concatenate([tail, rim]), "prow", pairs)
        tail = tail + got[: across - 1]
        rim = pick(rim_steps[-1], got[across - 1 :], rim)

    side = after(head, have2)
    for pairs in far_steps(nc):
        joint = [(i * nc + s, i * nc + t) for i in range(nr) for s, t in pairs if s % 2 != i % 2]
        got = lax.ppermute(side, joined, joint)
        right = member(my_col, pairs) & (my_col % 2 != my_row % 2)
        side = jnp.where(right, got, side)
    joint = [(i * nc + s, i * nc + (s ^ 1)) for i in range(nr) for s in range(nc) if s % 2 != i % 2]
    other1 = near(have1)
    side = jnp.where(my_col % 2 == my_row % 2, lax.ppermute(side, joined, joint), side)
    other2 = near(have2)

    args = [me, goes, lower_inverse, upper_inverse]
    parts = [flat, head, swap(head), tail, swap(tail), side, swap(side), top, swap(top), rim, swap(rim),
             have0, have1, have2, other0, other1, other2]
    return call(
        functools.partial(finish_kernel, nr, nc, len(parts)),
        shape(*matrix.shape),
        args + parts,
        [SMEM] + [VMEM] * 3 + [ANY] * len(parts),
        ANY,
        [pltpu.VMEM(p.shape, BF) for p in parts] +
        [pltpu.VMEM((across, 4 * block, width), BF)] + [pltpu.VMEM((block, width), BF)] * 4 +
        [pltpu.VMEM(matrix.shape, BF), pltpu.SemaphoreType.DMA((len(parts),)), pltpu.SemaphoreType.DMA((down,))],
    )


def solution(mesh):
    in_specs = (P(None, "prow", None, "pcol"), P(), P(), P())
    out_specs = P(None, "prow", None, "pcol")
    return jax.shard_map(local, mesh=mesh, in_specs=in_specs, out_specs=out_specs, check_vma=False)
```

```python
import functools

import jax
import jax.numpy as jnp
from jax import lax
from jax.experimental import pallas as pl
from jax.experimental.pallas import tpu as pltpu
from jax.sharding import PartitionSpec as P

BF, F32 = jnp.bfloat16, jnp.float32
VMEM = pl.BlockSpec(memory_space=pltpu.VMEM)
SMEM = pl.BlockSpec(memory_space=pltpu.SMEM)
ANY = pl.BlockSpec(memory_space=pl.ANY)
HBM = pl.BlockSpec(memory_space=pltpu.HBM)
WEIGHT = 10**11


def bits_of(count):
    return list(range(1, count.bit_length() - 1))


def exchange_pairs(count, level):
    order = bits_of(count)
    return [(i, i ^ (1 << (order[level] if i % 2 == 0 else order[-1 - level]))) for i in range(count)]


def spread_pairs(count, levels):
    held, steps = [0, 1], []
    for level in levels:
        pairs = [pair for pair in exchange_pairs(count, level) if pair[0] in held]
        held = held + [target for _, target in pairs]
        steps.append(pairs)
    return steps


def far_steps(count):
    steps = []
    distance = count // 2
    while distance >= 2:
        steps.append([(i, i + distance) for i in range(count) if i % (2 * distance) < 2])
        distance //= 2
    return steps


def twin(count):
    return [(i, i ^ 1) for i in range(count)]


def member(index, pairs):
    return sum((index == t).astype(jnp.int32) for _, t in pairs) > 0


def after(value, *others):
    return lax.optimization_barrier((value, *others))[0]


def dot(a, b):
    return jnp.dot(a, b, preferred_element_type=F32)


def call(body, outs, args, in_specs, out_specs, scratch=(), flops=10**6, limit=10):
    return pl.pallas_call(
        body,
        out_shape=outs,
        in_specs=in_specs,
        out_specs=out_specs,
        scratch_shapes=list(scratch),
        compiler_params=pltpu.CompilerParams(vmem_limit_bytes=limit << 20),
        cost_estimate=pl.CostEstimate(flops=flops, bytes_accessed=0, transcendentals=0),
    )(*args)


def first_kernel(a, piece, top, held, sem):
    copy = pltpu.make_async_copy(a.at[0], held, sem)
    copy.start()
    copy.wait()
    turned = jnp.transpose(held[...], (1, 0, 2))
    piece[...] = turned[0]
    top[...] = turned


def join_kernel(keep, got, top, out):
    across = keep.shape[0]
    out[:across] = keep[...] + got[...]
    out[across:] = top[...]


def merge_kernel(taken, part, got, out):
    across = part.shape[0] // 2
    out[:across] = part[:across] + got[:across]

    @pl.when(taken[0] > 0)
    def _():
        out[across:] = got[across:]

    @pl.when(taken[0] == 0)
    def _():
        out[across:] = part[across:]


def pick_kernel(nr, me, a, row, first_piece, keep, give, middle, last, goes,
                raw, turned, hot, raw_sems):
    down, block, across, width = a.shape
    for b in range(down):
        pltpu.make_async_copy(a.at[b], raw.at[b], raw_sems.at[b]).start()
    my_row = me[0]
    even = my_row % 2 == 0
    first, second = row[0:1], row[1:2]
    i = lax.broadcasted_iota(jnp.int32, (block, block), 0)
    j = lax.broadcasted_iota(jnp.int32, (block, block), 1)

    def stand(line):
        line = jnp.where(i == j, line.astype(F32), 0.0)
        return jnp.sum(line, axis=1, keepdims=True).astype(jnp.int32)

    first_down, second_down = stand(first), stand(second)

    def found(mask, value, axis):
        value = jnp.where(mask, value.astype(F32), 0.0)
        count = jnp.sum(mask.astype(F32), axis=axis, keepdims=True)
        return count > 0.5, jnp.sum(value, axis=axis, keepdims=True).astype(jnp.int32)

    same = second_down == first
    hit, at = found(same, j, 1)
    second_source = jnp.where(hit, at, second_down)
    hit, at = found(first == block + i, jnp.broadcast_to(second_down, i.shape), 0)
    first_goes = jnp.where(hit, at, first)
    hit, at = found(same, i, 0)
    goes[0:1, :block] = jnp.where(hit, block + at, first_goes)
    hit, at = found(first_down == block + j, i, 0)
    goes[0:1, block:] = jnp.where(hit, at, second)

    kept = jnp.where(even, first_down, second_source)
    given = jnp.where(even, second_source, first_down)
    for b in range(down):
        base = (b * nr + my_row) * block
        hot[:block, b * block : (b + 1) * block] = (kept - base == j).astype(BF)
        hot[block:, b * block : (b + 1) * block] = (given - base == j).astype(BF)
    for b in range(down):
        pltpu.make_async_copy(a.at[b], raw.at[b], raw_sems.at[b]).wait()
        turned[:, b] = jnp.transpose(raw[b], (1, 0, 2))
        if b == down - 1:
            last[...] = turned[0, b]
        elif b > 0:
            middle[b - 1] = turned[0, b]
    for c in range(across):
        picked = dot(hot[...], turned[c].reshape(down * block, width)).astype(BF)
        keep[c] = picked[:block]
        give[c] = picked[block:]


def turn_kernel(a, gate, out, raw, turned, raw_sems, sems):
    down = a.shape[0]
    for b in range(down):
        pltpu.make_async_copy(a.at[b], raw.at[b], raw_sems.at[b]).start()
    for b in range(down):
        pltpu.make_async_copy(a.at[b], raw.at[b], raw_sems.at[b]).wait()
        turned[:, b] = jnp.transpose(raw[b], (1, 0, 2))
        pltpu.make_async_copy(turned.at[:, b], out.at[:, b], sems.at[b]).start()
    for b in range(down):
        pltpu.make_async_copy(turned.at[:, b], out.at[:, b], sems.at[b]).wait()


def finish_kernel(nr, nc, parts, me, goes, lower, upper, *refs):
    flat, head_mine, head_other, tail_mine, tail_other, side_mine, side_other, top_mine, top_other, rim_mine, rim_other, have0, have1, have2, other0, other1, other2 = refs[:17]
    sources, rest = refs[17 : 17 + parts], refs[17 + parts :]
    out, held = rest[0], rest[1 : 1 + parts]
    mix, r0, r1, result, in_sems, sems = rest[1 + parts :]
    copies = [pltpu.make_async_copy(s, h, in_sems.at[k]) for k, (s, h) in enumerate(zip(sources, held))]
    for copy in copies:
        copy.start()
    have, other = (have0, have1, have2), (other0, other1, other2)
    across, down, block, width = flat.shape
    my_row, my_col = me[0], me[1]
    even = my_row % 2 == 0
    even_col = my_col % 2 == 0

    def both(mine, others):
        return jnp.where(even, mine, others), jnp.where(even, others, mine)

    side01, side10 = both(side_mine[...], side_other[...])
    u0p = dot(lower[0], side01).astype(BF)
    lp = dot(side10, upper[0]).astype(BF)
    for c in range(across):
        if c == 0:
            a0, a1 = both(head_mine[...], head_other[...])
        else:
            a0, a1 = both(tail_mine[c - 1], tail_other[c - 1])
        u = dot(lower[0], a0).astype(BF)
        a1 = (a1.astype(F32) - dot(lp, u)).astype(BF)
        if c == 0:
            r0[...] = a0
            r1[...] = a1
        t0, t1 = both(top_mine[c], top_other[c])
        mix[c, :block] = t0
        mix[c, block : 2 * block] = t1
        mix[c, 2 * block : 3 * block] = u
        mix[c, 3 * block :] = dot(lower[1], a1).astype(BF)
    rim = [jnp.concatenate(both(rim_mine[k], rim_other[k]), 0) for k in range(2)]
    for copy in copies:
        copy.wait()
    place = lax.broadcasted_iota(jnp.int32, (block, 2 * block), 0)
    half = max(down // 2, 1)
    for h in range(0, down, half):
        match = jnp.concatenate([goes[...] - (b * nr + my_row) * block == place for b in range(h, h + half)], 0)
        onehot = match.astype(BF)
        hit = jnp.sum(match.astype(F32), axis=1, keepdims=True) > 0.5

        def rows_of(three):
            first, middle, last = three
            picked = []
            for b in range(h, h + half):
                picked.append(first[...] if b == 0 else last[...] if b == down - 1 else middle[b - 1])
            return jnp.concatenate(picked, 0)

        mine, others = rows_of(have), rows_of(other)
        z0 = jnp.where(hit, dot(onehot, rim[0]).astype(BF), jnp.where(even_col, mine, others))
        z1 = jnp.where(hit, dot(onehot, rim[1]).astype(BF), jnp.where(even_col, others, mine))
        l0 = dot(z0, upper[0]).astype(BF)
        l1 = dot((z1.astype(F32) - dot(l0, u0p)).astype(BF), upper[1]).astype(BF)
        factors = jnp.concatenate([onehot, -l0, -l1], 1)
        blocks = []
        for c in range(across):
            kept = jnp.where(hit, jnp.zeros((), BF), flat[c, h : h + half].reshape(half * block, width))
            s = (kept.astype(F32) + dot(factors, mix[c])).astype(BF)
            if c == 0:
                s = jnp.where(my_col == 0, l0, jnp.where(my_col == 1, l1, s))
            blocks.append(s)
        for b in range(h, h + half):
            held_rows = slice((b - h) * block, (b - h + 1) * block)
            tiles = [s[held_rows] for s in blocks]
            if b == 0:
                for c in range(across):
                    w0, w1 = mix[c, 2 * block : 3 * block], mix[c, 3 * block :]
                    if c == 0:
                        w0 = jnp.where(my_col == 0, r0[...], w0)
                        w1 = jnp.where(my_col == 0, lp, jnp.where(my_col == 1, r1[...], w1))
                    tiles[c] = jnp.where(my_row == 0, w0, jnp.where(my_row == 1, w1, tiles[c]))
            result[b] = jnp.transpose(jnp.stack(tiles), (1, 0, 2))
            pltpu.make_async_copy(result.at[b], out.at[b], sems.at[b]).start()
    for b in range(down):
        pltpu.make_async_copy(result.at[b], out.at[b], sems.at[b]).wait()


def local(matrix, pivots, lower_inverse, upper_inverse):
    nr = lax.axis_size("prow")
    nc = lax.axis_size("pcol")
    my_row = lax.axis_index("prow")
    my_col = lax.axis_index("pcol")
    down, block, across, width = matrix.shape
    joined = ("prow", "pcol")
    me = jnp.stack([my_row, my_col]).astype(jnp.int32)
    even_col = my_col % 2 == 0
    shape = lambda *s: jax.ShapeDtypeStruct(s, BF)
    depth = len(bits_of(nr))
    top_steps = spread_pairs(nr, [depth - 1] + list(range(depth - 1)) if depth else [])
    rim_steps = spread_pairs(nr, list(range(depth)))

    def far(piece):
        for pairs in far_steps(nc):
            got = lax.ppermute(piece, "pcol", pairs)
            piece = jnp.where(member(my_col, pairs), got, piece)
        return piece

    def near(piece):
        return lax.ppermute(piece, "pcol", twin(nc))

    def swap(part):
        return lax.ppermute(part, "prow", twin(nr))

    def pick(pairs, got, part):
        return jnp.where(member(my_row, pairs), got, part)

    first_piece, top = call(
        first_kernel, [shape(block, width), shape(across, block, width)], [matrix], [HBM], [VMEM] * 2,
        [pltpu.VMEM((block, across, width), BF), pltpu.SemaphoreType.DMA], limit=4,
    )
    have0 = far(first_piece)
    for pairs in top_steps[:1]:
        top = pick(pairs, lax.ppermute(top, "prow", pairs), top)

    keep, give, middle, last, goes = call(
        functools.partial(pick_kernel, nr),
        [shape(across, block, width),
         shape(across, block, width), shape(down - 2, block, width), shape(block, width),
         jax.ShapeDtypeStruct((1, 2 * block), jnp.int32)],
        [me, matrix, pivots, first_piece],
        [SMEM, HBM, VMEM, ANY],
        [VMEM] * 5,
        [pltpu.VMEM(matrix.shape, BF), pltpu.VMEM((across, down, block, width), BF),
         pltpu.VMEM((2 * block, down * block), BF),
         pltpu.SemaphoreType.DMA((down,))],
    )
    have1, have2 = far(middle), far(last)
    other0 = near(after(have0, keep))
    rim = jnp.stack([jnp.where(even_col, have0, other0), jnp.where(even_col, other0, have0)])

    part = call(
        join_kernel, shape(2 * across, block, width), [keep, swap(after(give, have0)), top], [VMEM] * 3, VMEM, flops=WEIGHT
    )
    flat = call(
        turn_kernel, shape(across, down, block, width), [matrix, other0], [HBM, ANY], HBM,
        [pltpu.VMEM(matrix.shape, BF), pltpu.VMEM((across, down, block, width), BF),
         pltpu.SemaphoreType.DMA((down,)), pltpu.SemaphoreType.DMA((down,))], flops=10**9, limit=16,
    )
    for pairs in rim_steps[:-1]:
        rim = pick(pairs, lax.ppermute(after(rim, have1, flat), "prow", pairs), rim)
    for level in range(depth - 1):
        pairs = exchange_pairs(nr, level)
        taken = member(my_row, top_steps[level + 1]).astype(jnp.int32)[None]
        part = call(
            merge_kernel, shape(2 * across, block, width), [taken, part, lax.ppermute(part, "prow", pairs)],
            [SMEM, VMEM, VMEM], VMEM, flops=WEIGHT,
        )
    head, tail, top = part[0], part[1:across], part[across:]
    if depth > 0:
        pairs = exchange_pairs(nr, depth - 1)
        head = head + lax.ppermute(head, "prow", pairs)
        got = lax.ppermute(jnp.concatenate([tail, rim]), "prow", pairs)
        tail = tail + got[: across - 1]
        rim = pick(rim_steps[-1], got[across - 1 :], rim)

    other1 = near(have1)
    side = after(head, have2, other1)
    for pairs in far_steps(nc):
        joint = [(i * nc + s, i * nc + t) for i in range(nr) for s, t in pairs if s % 2 != i % 2]
        got = lax.ppermute(side, joined, joint)
        right = member(my_col, pairs) & (my_col % 2 != my_row % 2)
        side = jnp.where(right, got, side)
    joint = [(i * nc + s, i * nc + (s ^ 1)) for i in range(nr) for s in range(nc) if s % 2 != i % 2]
    side = jnp.where(my_col % 2 == my_row % 2, lax.ppermute(side, joined, joint), side)
    other2 = near(have2)

    args = [me, goes, lower_inverse, upper_inverse]
    ready = [flat, head, swap(head), tail, swap(tail), side, swap(side), top, swap(top), rim, swap(rim), have0, have1, have2, other0, other1, other2]
    parts = []
    return call(
        functools.partial(finish_kernel, nr, nc, len(parts)),
        shape(*matrix.shape),
        args + ready + parts,
        [SMEM] + [VMEM] * (3 + len(ready)) + [ANY] * len(parts),
        ANY,
        [pltpu.VMEM(p.shape, BF) for p in parts] +
        [pltpu.VMEM((across, 4 * block, width), BF)] + [pltpu.VMEM((block, width), BF)] * 2 +
        [pltpu.VMEM(matrix.shape, BF), pltpu.SemaphoreType.DMA((max(len(parts), 1),)), pltpu.SemaphoreType.DMA((down,))],
        limit=12,
    )


def solution(mesh):
    in_specs = (P(None, "prow", None, "pcol"), P(), P(), P())
    out_specs = P(None, "prow", None, "pcol")
    return jax.shard_map(local, mesh=mesh, in_specs=in_specs, out_specs=out_specs, check_vma=False)
```

```python
import functools

import jax
import jax.numpy as jnp
from jax import lax
from jax.experimental import pallas as pl
from jax.experimental.pallas import tpu as pltpu
from jax.sharding import PartitionSpec as P

BF, F32 = jnp.bfloat16, jnp.float32
VMEM = pl.BlockSpec(memory_space=pltpu.VMEM)
SMEM = pl.BlockSpec(memory_space=pltpu.SMEM)
ANY = pl.BlockSpec(memory_space=pl.ANY)
HBM = pl.BlockSpec(memory_space=pltpu.HBM)
WEIGHT = 10**11


def bits_of(count):
    return list(range(1, count.bit_length() - 1))


def exchange_pairs(count, level):
    order = bits_of(count)
    return [(i, i ^ (1 << (order[level] if i % 2 == 0 else order[-1 - level]))) for i in range(count)]


def spread_pairs(count, levels):
    held, steps = [0, 1], []
    for level in levels:
        pairs = [pair for pair in exchange_pairs(count, level) if pair[0] in held]
        held = held + [target for _, target in pairs]
        steps.append(pairs)
    return steps


def far_steps(count):
    steps = []
    distance = count // 2
    while distance >= 2:
        steps.append([(i, i + distance) for i in range(count) if i % (2 * distance) < 2])
        distance //= 2
    return steps


def twin(count):
    return [(i, i ^ 1) for i in range(count)]


def member(index, pairs):
    return sum((index == t).astype(jnp.int32) for _, t in pairs) > 0


def after(value, *others):
    return lax.optimization_barrier((value, *others))[0]


def dot(a, b):
    return jnp.dot(a, b, preferred_element_type=F32)


def call(body, outs, args, in_specs, out_specs, scratch=(), flops=10**6, limit=10):
    return pl.pallas_call(
        body,
        out_shape=outs,
        in_specs=in_specs,
        out_specs=out_specs,
        scratch_shapes=list(scratch),
        compiler_params=pltpu.CompilerParams(vmem_limit_bytes=limit << 20),
        cost_estimate=pl.CostEstimate(flops=flops, bytes_accessed=0, transcendentals=0),
    )(*args)


def first_kernel(a, piece, top, held, sem):
    copy = pltpu.make_async_copy(a.at[0], held, sem)
    copy.start()
    copy.wait()
    turned = jnp.transpose(held[...], (1, 0, 2))
    piece[...] = turned[0]
    top[...] = turned


def join_kernel(keep, got, top, out):
    across = keep.shape[0]
    out[:across] = keep[...] + got[...]
    out[across:] = top[...]


def merge_kernel(taken, part, got, out):
    across = part.shape[0] // 2
    out[:across] = part[:across] + got[:across]

    @pl.when(taken[0] > 0)
    def _():
        out[across:] = got[across:]

    @pl.when(taken[0] == 0)
    def _():
        out[across:] = part[across:]


def pick_kernel(nr, me, a, row, first_piece, keep, give, middle, last, goes,
                raw, turned, hot, raw_sems):
    down, block, across, width = a.shape
    for b in range(down):
        pltpu.make_async_copy(a.at[b], raw.at[b], raw_sems.at[b]).start()
    my_row = me[0]
    even = my_row % 2 == 0
    first, second = row[0:1], row[1:2]
    i = lax.broadcasted_iota(jnp.int32, (block, block), 0)
    j = lax.broadcasted_iota(jnp.int32, (block, block), 1)

    def stand(line):
        line = jnp.where(i == j, line.astype(F32), 0.0)
        return jnp.sum(line, axis=1, keepdims=True).astype(jnp.int32)

    first_down, second_down = stand(first), stand(second)

    def found(mask, value, axis):
        value = jnp.where(mask, value.astype(F32), 0.0)
        count = jnp.sum(mask.astype(F32), axis=axis, keepdims=True)
        return count > 0.5, jnp.sum(value, axis=axis, keepdims=True).astype(jnp.int32)

    same = second_down == first
    hit, at = found(same, j, 1)
    second_source = jnp.where(hit, at, second_down)
    hit, at = found(first == block + i, jnp.broadcast_to(second_down, i.shape), 0)
    first_goes = jnp.where(hit, at, first)
    hit, at = found(same, i, 0)
    goes[0:1, :block] = jnp.where(hit, block + at, first_goes)
    hit, at = found(first_down == block + j, i, 0)
    goes[0:1, block:] = jnp.where(hit, at, second)

    kept = jnp.where(even, first_down, second_source)
    given = jnp.where(even, second_source, first_down)
    for b in range(down):
        base = (b * nr + my_row) * block
        hot[:block, b * block : (b + 1) * block] = (kept - base == j).astype(BF)
        hot[block:, b * block : (b + 1) * block] = (given - base == j).astype(BF)
    for b in range(down):
        pltpu.make_async_copy(a.at[b], raw.at[b], raw_sems.at[b]).wait()
        turned[:, b] = jnp.transpose(raw[b], (1, 0, 2))
        if b == down - 1:
            last[...] = turned[0, b]
        elif b > 0:
            middle[b - 1] = turned[0, b]
    for c in range(across):
        picked = dot(hot[...], turned[c].reshape(down * block, width)).astype(BF)
        keep[c] = picked[:block]
        give[c] = picked[block:]


def turn_kernel(a, gate, out, raw, turned, raw_sems, sems):
    down = a.shape[0]
    for b in range(down):
        pltpu.make_async_copy(a.at[b], raw.at[b], raw_sems.at[b]).start()
    for b in range(down):
        pltpu.make_async_copy(a.at[b], raw.at[b], raw_sems.at[b]).wait()
        turned[:, b] = jnp.transpose(raw[b], (1, 0, 2))
        pltpu.make_async_copy(turned.at[:, b], out.at[:, b], sems.at[b]).start()
    for b in range(down):
        pltpu.make_async_copy(turned.at[:, b], out.at[:, b], sems.at[b]).wait()


def finish_kernel(nr, nc, parts, me, goes, lower, upper, *refs):
    flat, head_mine, head_other, tail_mine, tail_other, side_mine, side_other, top_mine, top_other, rim_mine, rim_other, have0, have1, have2, other0, other1, other2 = refs[:17]
    sources, rest = refs[17 : 17 + parts], refs[17 + parts :]
    out, held = rest[0], rest[1 : 1 + parts]
    mix, r0, r1, result, in_sems, sems = rest[1 + parts :]
    copies = [pltpu.make_async_copy(s, h, in_sems.at[k]) for k, (s, h) in enumerate(zip(sources, held))]
    for copy in copies:
        copy.start()
    have, other = (have0, have1, have2), (other0, other1, other2)
    across, down, block, width = flat.shape
    my_row, my_col = me[0], me[1]
    even = my_row % 2 == 0
    even_col = my_col % 2 == 0

    def both(mine, others):
        return jnp.where(even, mine, others), jnp.where(even, others, mine)

    side01, side10 = both(side_mine[...], side_other[...])
    u0p = dot(lower[0], side01).astype(BF)
    lp = dot(side10, upper[0]).astype(BF)
    heads = [both(head_mine[...], head_other[...])]
    heads += [both(tail_mine[c], tail_other[c]) for c in range(across - 1)]
    firsts = [dot(lower[0], a0).astype(BF) for a0, _ in heads]
    seconds = [(a1.astype(F32) - dot(lp, u)).astype(BF) for (_, a1), u in zip(heads, firsts)]
    r0[...] = heads[0][0]
    r1[...] = seconds[0]
    for c in range(across):
        t0, t1 = both(top_mine[c], top_other[c])
        mix[c, :block] = t0
        mix[c, block : 2 * block] = t1
        mix[c, 2 * block : 3 * block] = firsts[c]
        mix[c, 3 * block :] = dot(lower[1], seconds[c]).astype(BF)
    rim = [jnp.concatenate(both(rim_mine[k], rim_other[k]), 0) for k in range(2)]
    for copy in copies:
        copy.wait()
    place = lax.broadcasted_iota(jnp.int32, (block, 2 * block), 0)
    half = down
    for h in range(0, down, half):
        match = jnp.concatenate([goes[...] - (b * nr + my_row) * block == place for b in range(h, h + half)], 0)
        onehot = match.astype(BF)
        hit = jnp.sum(match.astype(F32), axis=1, keepdims=True) > 0.5

        def rows_of(three):
            first, middle, last = three
            picked = []
            for b in range(h, h + half):
                picked.append(first[...] if b == 0 else last[...] if b == down - 1 else middle[b - 1])
            return jnp.concatenate(picked, 0)

        mine, others = rows_of(have), rows_of(other)
        z0 = jnp.where(hit, dot(onehot, rim[0]).astype(BF), jnp.where(even_col, mine, others))
        z1 = jnp.where(hit, dot(onehot, rim[1]).astype(BF), jnp.where(even_col, others, mine))
        l0 = dot(z0, upper[0]).astype(BF)
        l1 = dot((z1.astype(F32) - dot(l0, u0p)).astype(BF), upper[1]).astype(BF)
        factors = jnp.concatenate([onehot, -l0, -l1], 1)
        blocks = []
        for c in range(across):
            kept = jnp.where(hit, jnp.zeros((), BF), flat[c, h : h + half].reshape(half * block, width))
            s = (kept.astype(F32) + dot(factors, mix[c])).astype(BF)
            if c == 0:
                s = jnp.where(my_col == 0, l0, jnp.where(my_col == 1, l1, s))
            blocks.append(s)
        for b in range(h, h + half):
            held_rows = slice((b - h) * block, (b - h + 1) * block)
            tiles = [s[held_rows] for s in blocks]
            if b == 0:
                for c in range(across):
                    w0, w1 = mix[c, 2 * block : 3 * block], mix[c, 3 * block :]
                    if c == 0:
                        w0 = jnp.where(my_col == 0, r0[...], w0)
                        w1 = jnp.where(my_col == 0, lp, jnp.where(my_col == 1, r1[...], w1))
                    tiles[c] = jnp.where(my_row == 0, w0, jnp.where(my_row == 1, w1, tiles[c]))
            result[b] = jnp.transpose(jnp.stack(tiles), (1, 0, 2))
            pltpu.make_async_copy(result.at[b], out.at[b], sems.at[b]).start()
    for b in range(down):
        pltpu.make_async_copy(result.at[b], out.at[b], sems.at[b]).wait()


def local(matrix, pivots, lower_inverse, upper_inverse):
    nr = lax.axis_size("prow")
    nc = lax.axis_size("pcol")
    my_row = lax.axis_index("prow")
    my_col = lax.axis_index("pcol")
    down, block, across, width = matrix.shape
    joined = ("prow", "pcol")
    me = jnp.stack([my_row, my_col]).astype(jnp.int32)
    even_col = my_col % 2 == 0
    shape = lambda *s: jax.ShapeDtypeStruct(s, BF)
    depth = len(bits_of(nr))
    top_steps = spread_pairs(nr, [depth - 1] + list(range(depth - 1)) if depth else [])
    rim_steps = spread_pairs(nr, list(range(depth)))

    def far(piece):
        for pairs in far_steps(nc):
            got = lax.ppermute(piece, "pcol", pairs)
            piece = jnp.where(member(my_col, pairs), got, piece)
        return piece

    def near(piece):
        return lax.ppermute(piece, "pcol", twin(nc))

    def swap(part):
        return lax.ppermute(part, "prow", twin(nr))

    def pick(pairs, got, part):
        return jnp.where(member(my_row, pairs), got, part)

    first_piece, top = call(
        first_kernel, [shape(block, width), shape(across, block, width)], [matrix], [HBM], [VMEM] * 2,
        [pltpu.VMEM((block, across, width), BF), pltpu.SemaphoreType.DMA], limit=4,
    )
    have0 = far(first_piece)
    for pairs in top_steps[:1]:
        top = pick(pairs, lax.ppermute(top, "prow", pairs), top)

    keep, give, middle, last, goes = call(
        functools.partial(pick_kernel, nr),
        [shape(across, block, width),
         shape(across, block, width), shape(down - 2, block, width), shape(block, width),
         jax.ShapeDtypeStruct((1, 2 * block), jnp.int32)],
        [me, matrix, pivots, first_piece],
        [SMEM, HBM, VMEM, ANY],
        [VMEM] * 5,
        [pltpu.VMEM(matrix.shape, BF), pltpu.VMEM((across, down, block, width), BF),
         pltpu.VMEM((2 * block, down * block), BF),
         pltpu.SemaphoreType.DMA((down,))],
    )
    have1, have2 = far(middle), far(last)
    other0 = near(after(have0, keep))
    rim = jnp.stack([jnp.where(even_col, have0, other0), jnp.where(even_col, other0, have0)])

    part = call(
        join_kernel, shape(2 * across, block, width), [keep, swap(after(give, have0)), top], [VMEM] * 3, VMEM, flops=WEIGHT
    )
    flat = call(
        turn_kernel, shape(across, down, block, width), [matrix, other0], [HBM, ANY], HBM,
        [pltpu.VMEM(matrix.shape, BF), pltpu.VMEM((across, down, block, width), BF),
         pltpu.SemaphoreType.DMA((down,)), pltpu.SemaphoreType.DMA((down,))], flops=10**9, limit=16,
    )
    for pairs in rim_steps[:-1]:
        rim = pick(pairs, lax.ppermute(after(rim, have1, flat), "prow", pairs), rim)
    for level in range(depth - 1):
        pairs = exchange_pairs(nr, level)
        taken = member(my_row, top_steps[level + 1]).astype(jnp.int32)[None]
        part = call(
            merge_kernel, shape(2 * across, block, width), [taken, part, lax.ppermute(part, "prow", pairs)],
            [SMEM, VMEM, VMEM], VMEM, flops=WEIGHT,
        )
    head, tail, top = part[0], part[1:across], part[across:]
    if depth > 0:
        pairs = exchange_pairs(nr, depth - 1)
        head = head + lax.ppermute(head, "prow", pairs)
        got = lax.ppermute(jnp.concatenate([tail, rim]), "prow", pairs)
        tail = tail + got[: across - 1]
        rim = pick(rim_steps[-1], got[across - 1 :], rim)

    other1 = near(have1)
    side = after(head, have2, other1)
    for pairs in far_steps(nc):
        joint = [(i * nc + s, i * nc + t) for i in range(nr) for s, t in pairs if s % 2 != i % 2]
        got = lax.ppermute(side, joined, joint)
        right = member(my_col, pairs) & (my_col % 2 != my_row % 2)
        side = jnp.where(right, got, side)
    far_side = side
    joint = [(i * nc + s, i * nc + (s ^ 1)) for i in range(nr) for s in range(nc) if s % 2 != i % 2]
    side = jnp.where(my_col % 2 == my_row % 2, lax.ppermute(side, joined, joint), side)
    other2 = near(after(have2, far_side))

    args = [me, goes, lower_inverse, upper_inverse]
    ready = [flat, head, swap(head), tail, swap(tail), side, swap(side), top, swap(top), rim, swap(rim), have0, have1, have2, other0, other1, other2]
    parts = []
    return call(
        functools.partial(finish_kernel, nr, nc, len(parts)),
        shape(*matrix.shape),
        args + ready + parts,
        [SMEM] + [VMEM] * (3 + len(ready)) + [ANY] * len(parts),
        ANY,
        [pltpu.VMEM(p.shape, BF) for p in parts] +
        [pltpu.VMEM((across, 4 * block, width), BF)] + [pltpu.VMEM((block, width), BF)] * 2 +
        [pltpu.VMEM(matrix.shape, BF), pltpu.SemaphoreType.DMA((max(len(parts), 1),)), pltpu.SemaphoreType.DMA((down,))],
        limit=12,
    )


def solution(mesh):
    in_specs = (P(None, "prow", None, "pcol"), P(), P(), P())
    out_specs = P(None, "prow", None, "pcol")
    return jax.shard_map(local, mesh=mesh, in_specs=in_specs, out_specs=out_specs, check_vma=False)
```

```python
import functools

import jax
import jax.numpy as jnp
from jax import lax
from jax.experimental import pallas as pl
from jax.experimental.pallas import tpu as pltpu
from jax.sharding import PartitionSpec as P

BF, F32 = jnp.bfloat16, jnp.float32
VMEM = pl.BlockSpec(memory_space=pltpu.VMEM)
SMEM = pl.BlockSpec(memory_space=pltpu.SMEM)
ANY = pl.BlockSpec(memory_space=pl.ANY)
HBM = pl.BlockSpec(memory_space=pltpu.HBM)
WEIGHT = 10**11


def bits_of(count):
    return list(range(1, count.bit_length() - 1))


def exchange_pairs(count, level):
    order = bits_of(count)
    return [(i, i ^ (1 << (order[level] if i % 2 == 0 else order[-1 - level]))) for i in range(count)]


def spread_pairs(count, levels):
    held, steps = [0, 1], []
    for level in levels:
        pairs = [pair for pair in exchange_pairs(count, level) if pair[0] in held]
        held = held + [target for _, target in pairs]
        steps.append(pairs)
    return steps


def far_steps(count):
    steps = []
    distance = count // 2
    while distance >= 2:
        steps.append([(i, i + distance) for i in range(count) if i % (2 * distance) < 2])
        distance //= 2
    return steps


def twin(count):
    return [(i, i ^ 1) for i in range(count)]


def member(index, pairs):
    return sum((index == t).astype(jnp.int32) for _, t in pairs) > 0


def after(value, *others):
    return lax.optimization_barrier((value, *others))[0]


def dot(a, b):
    return jnp.dot(a, b, preferred_element_type=F32)


def call(body, outs, args, in_specs, out_specs, scratch=(), flops=10**6, limit=10):
    return pl.pallas_call(
        body,
        out_shape=outs,
        in_specs=in_specs,
        out_specs=out_specs,
        scratch_shapes=list(scratch),
        compiler_params=pltpu.CompilerParams(vmem_limit_bytes=limit << 20),
        cost_estimate=pl.CostEstimate(flops=flops, bytes_accessed=0, transcendentals=0),
    )(*args)


def first_kernel(a, piece, top, held, sem):
    copy = pltpu.make_async_copy(a.at[0], held, sem)
    copy.start()
    copy.wait()
    turned = jnp.transpose(held[...], (1, 0, 2))
    piece[...] = turned[0]
    top[...] = turned


def join_kernel(keep, got, top, out):
    across = keep.shape[0]
    out[:across] = keep[...] + got[...]
    out[across:] = top[...]


def merge_kernel(taken, part, got, out):
    across = part.shape[0] // 2
    out[:across] = part[:across] + got[:across]

    @pl.when(taken[0] > 0)
    def _():
        out[across:] = got[across:]

    @pl.when(taken[0] == 0)
    def _():
        out[across:] = part[across:]


def pick_kernel(nr, me, a, row, first_piece, keep, give, middle, last, goes,
                turned, hot):
    down, block, across, width = a.shape
    my_row = me[0]
    even = my_row % 2 == 0
    first, second = row[0:1], row[1:2]
    i = lax.broadcasted_iota(jnp.int32, (block, block), 0)
    j = lax.broadcasted_iota(jnp.int32, (block, block), 1)

    def stand(line):
        line = jnp.where(i == j, line.astype(F32), 0.0)
        return jnp.sum(line, axis=1, keepdims=True).astype(jnp.int32)

    first_down, second_down = stand(first), stand(second)

    def found(mask, value, axis):
        value = jnp.where(mask, value.astype(F32), 0.0)
        count = jnp.sum(mask.astype(F32), axis=axis, keepdims=True)
        return count > 0.5, jnp.sum(value, axis=axis, keepdims=True).astype(jnp.int32)

    same = second_down == first
    hit, at = found(same, j, 1)
    second_source = jnp.where(hit, at, second_down)
    hit, at = found(first == block + i, jnp.broadcast_to(second_down, i.shape), 0)
    first_goes = jnp.where(hit, at, first)
    hit, at = found(same, i, 0)
    goes[0:1, :block] = jnp.where(hit, block + at, first_goes)
    hit, at = found(first_down == block + j, i, 0)
    goes[0:1, block:] = jnp.where(hit, at, second)

    kept = jnp.where(even, first_down, second_source)
    given = jnp.where(even, second_source, first_down)
    for b in range(down):
        base = (b * nr + my_row) * block
        hot[:block, b * block : (b + 1) * block] = (kept - base == j).astype(BF)
        hot[block:, b * block : (b + 1) * block] = (given - base == j).astype(BF)
    for b in range(down):
        turned[:, b] = jnp.transpose(a[b], (1, 0, 2))
        if b == down - 1:
            last[...] = turned[0, b]
        elif b > 0:
            middle[b - 1] = turned[0, b]
    for c in range(across):
        picked = dot(hot[...], turned[c].reshape(down * block, width)).astype(BF)
        keep[c] = picked[:block]
        give[c] = picked[block:]


def turn_kernel(a, gate, out, raw, turned, raw_sems, sems):
    down = a.shape[0]
    for b in range(down):
        pltpu.make_async_copy(a.at[b], raw.at[b], raw_sems.at[b]).start()
    for b in range(down):
        pltpu.make_async_copy(a.at[b], raw.at[b], raw_sems.at[b]).wait()
        turned[:, b] = jnp.transpose(raw[b], (1, 0, 2))
        pltpu.make_async_copy(turned.at[:, b], out.at[:, b], sems.at[b]).start()
    for b in range(down):
        pltpu.make_async_copy(turned.at[:, b], out.at[:, b], sems.at[b]).wait()


def finish_kernel(nr, nc, parts, me, goes, lower, upper, *refs):
    flat, head_mine, head_other, tail_mine, tail_other, side_mine, side_other, top_mine, top_other, rim_mine, rim_other, have0, have1, have2, other0, other1, other2 = refs[:17]
    sources, rest = refs[17 : 17 + parts], refs[17 + parts :]
    out, held = rest[0], rest[1 : 1 + parts]
    mix, r0, r1, result, in_sems, sems = rest[1 + parts :]
    copies = [pltpu.make_async_copy(s, h, in_sems.at[k]) for k, (s, h) in enumerate(zip(sources, held))]
    for copy in copies:
        copy.start()
    have, other = (have0, have1, have2), (other0, other1, other2)
    across, down, block, width = flat.shape
    my_row, my_col = me[0], me[1]
    even = my_row % 2 == 0
    even_col = my_col % 2 == 0

    def both(mine, others):
        return jnp.where(even, mine, others), jnp.where(even, others, mine)

    side01, side10 = both(side_mine[...], side_other[...])
    u0p = dot(lower[0], side01).astype(BF)
    lp = dot(side10, upper[0]).astype(BF)
    heads = [both(head_mine[...], head_other[...])]
    heads += [both(tail_mine[c], tail_other[c]) for c in range(across - 1)]
    firsts = [dot(lower[0], a0).astype(BF) for a0, _ in heads]
    seconds = [(a1.astype(F32) - dot(lp, u)).astype(BF) for (_, a1), u in zip(heads, firsts)]
    r0[...] = heads[0][0]
    r1[...] = seconds[0]
    for c in range(across):
        t0, t1 = both(top_mine[c], top_other[c])
        mix[c, :block] = t0
        mix[c, block : 2 * block] = t1
        mix[c, 2 * block : 3 * block] = firsts[c]
        mix[c, 3 * block :] = dot(lower[1], seconds[c]).astype(BF)
    rim = [jnp.concatenate(both(rim_mine[k], rim_other[k]), 0) for k in range(2)]
    for copy in copies:
        copy.wait()
    place = lax.broadcasted_iota(jnp.int32, (block, 2 * block), 0)
    half = down
    for h in range(0, down, half):
        match = jnp.concatenate([goes[...] - (b * nr + my_row) * block == place for b in range(h, h + half)], 0)
        onehot = match.astype(BF)
        hit = jnp.sum(match.astype(F32), axis=1, keepdims=True) > 0.5

        def rows_of(three):
            first, middle, last = three
            picked = []
            for b in range(h, h + half):
                picked.append(first[...] if b == 0 else last[...] if b == down - 1 else middle[b - 1])
            return jnp.concatenate(picked, 0)

        mine, others = rows_of(have), rows_of(other)
        z0 = jnp.where(hit, dot(onehot, rim[0]).astype(BF), jnp.where(even_col, mine, others))
        z1 = jnp.where(hit, dot(onehot, rim[1]).astype(BF), jnp.where(even_col, others, mine))
        l0 = dot(z0, upper[0]).astype(BF)
        l1 = dot((z1.astype(F32) - dot(l0, u0p)).astype(BF), upper[1]).astype(BF)
        factors = jnp.concatenate([onehot, -l0, -l1], 1)
        blocks = []
        for c in range(across):
            kept = jnp.where(hit, jnp.zeros((), BF), flat[c, h : h + half].reshape(half * block, width))
            s = (kept.astype(F32) + dot(factors, mix[c])).astype(BF)
            if c == 0:
                s = jnp.where(my_col == 0, l0, jnp.where(my_col == 1, l1, s))
            blocks.append(s)
        for b in range(h, h + half):
            held_rows = slice((b - h) * block, (b - h + 1) * block)
            tiles = [s[held_rows] for s in blocks]
            if b == 0:
                for c in range(across):
                    w0, w1 = mix[c, 2 * block : 3 * block], mix[c, 3 * block :]
                    if c == 0:
                        w0 = jnp.where(my_col == 0, r0[...], w0)
                        w1 = jnp.where(my_col == 0, lp, jnp.where(my_col == 1, r1[...], w1))
                    tiles[c] = jnp.where(my_row == 0, w0, jnp.where(my_row == 1, w1, tiles[c]))
            result[b] = jnp.transpose(jnp.stack(tiles), (1, 0, 2))
            pltpu.make_async_copy(result.at[b], out.at[b], sems.at[b]).start()
    for b in range(down):
        pltpu.make_async_copy(result.at[b], out.at[b], sems.at[b]).wait()


def local(matrix, pivots, lower_inverse, upper_inverse):
    nr = lax.axis_size("prow")
    nc = lax.axis_size("pcol")
    my_row = lax.axis_index("prow")
    my_col = lax.axis_index("pcol")
    down, block, across, width = matrix.shape
    joined = ("prow", "pcol")
    me = jnp.stack([my_row, my_col]).astype(jnp.int32)
    even_col = my_col % 2 == 0
    shape = lambda *s: jax.ShapeDtypeStruct(s, BF)
    depth = len(bits_of(nr))
    top_steps = spread_pairs(nr, [depth - 1] + list(range(depth - 1)) if depth else [])
    rim_steps = spread_pairs(nr, list(range(depth)))

    def far(piece):
        for pairs in far_steps(nc):
            got = lax.ppermute(piece, "pcol", pairs)
            piece = jnp.where(member(my_col, pairs), got, piece)
        return piece

    def near(piece):
        return lax.ppermute(piece, "pcol", twin(nc))

    def swap(part):
        return lax.ppermute(part, "prow", twin(nr))

    def pick(pairs, got, part):
        return jnp.where(member(my_row, pairs), got, part)

    first_piece, top = call(
        first_kernel, [shape(block, width), shape(across, block, width)], [matrix], [HBM], [VMEM] * 2,
        [pltpu.VMEM((block, across, width), BF), pltpu.SemaphoreType.DMA], limit=4,
    )
    have0 = far(first_piece)
    for pairs in top_steps[:1]:
        top = pick(pairs, lax.ppermute(top, "prow", pairs), top)

    keep, give, middle, last, goes = call(
        functools.partial(pick_kernel, nr),
        [shape(across, block, width),
         shape(across, block, width), shape(down - 2, block, width), shape(block, width),
         jax.ShapeDtypeStruct((1, 2 * block), jnp.int32)],
        [me, matrix, pivots, first_piece],
        [SMEM, VMEM, VMEM, ANY],
        [VMEM] * 5,
        [pltpu.VMEM((across, down, block, width), BF),
         pltpu.VMEM((2 * block, down * block), BF)],
    )
    have1, have2 = far(middle), far(last)
    other0 = near(after(have0, keep))
    rim = jnp.stack([jnp.where(even_col, have0, other0), jnp.where(even_col, other0, have0)])

    part = call(
        join_kernel, shape(2 * across, block, width), [keep, swap(after(give, have0)), top], [VMEM] * 3, VMEM, flops=WEIGHT
    )
    flat = call(
        turn_kernel, shape(across, down, block, width), [matrix, other0], [HBM, ANY], HBM,
        [pltpu.VMEM(matrix.shape, BF), pltpu.VMEM((across, down, block, width), BF),
         pltpu.SemaphoreType.DMA((down,)), pltpu.SemaphoreType.DMA((down,))], flops=10**9, limit=16,
    )
    for pairs in rim_steps[:-1]:
        rim = pick(pairs, lax.ppermute(after(rim, have1, flat), "prow", pairs), rim)
    for level in range(depth - 1):
        pairs = exchange_pairs(nr, level)
        taken = member(my_row, top_steps[level + 1]).astype(jnp.int32)[None]
        part = call(
            merge_kernel, shape(2 * across, block, width), [taken, part, lax.ppermute(part, "prow", pairs)],
            [SMEM, VMEM, VMEM], VMEM, flops=WEIGHT,
        )
    head, tail, top = part[0], part[1:across], part[across:]
    if depth > 0:
        pairs = exchange_pairs(nr, depth - 1)
        head = head + lax.ppermute(head, "prow", pairs)
        got = lax.ppermute(jnp.concatenate([tail, rim]), "prow", pairs)
        tail = tail + got[: across - 1]
        rim = pick(rim_steps[-1], got[across - 1 :], rim)

    other1 = near(have1)
    side = after(head, have2, other1)
    for pairs in far_steps(nc):
        joint = [(i * nc + s, i * nc + t) for i in range(nr) for s, t in pairs if s % 2 != i % 2]
        got = lax.ppermute(side, joined, joint)
        right = member(my_col, pairs) & (my_col % 2 != my_row % 2)
        side = jnp.where(right, got, side)
    far_side = side
    joint = [(i * nc + s, i * nc + (s ^ 1)) for i in range(nr) for s in range(nc) if s % 2 != i % 2]
    side = jnp.where(my_col % 2 == my_row % 2, lax.ppermute(side, joined, joint), side)
    other2 = near(after(have2, far_side))

    args = [me, goes, lower_inverse, upper_inverse]
    ready = [flat, head, swap(head), tail, swap(tail), side, swap(side), top, swap(top), rim, swap(rim), have0, have1, have2, other0, other1, other2]
    parts = []
    return call(
        functools.partial(finish_kernel, nr, nc, len(parts)),
        shape(*matrix.shape),
        args + ready + parts,
        [SMEM] + [VMEM] * (3 + len(ready)) + [ANY] * len(parts),
        ANY,
        [pltpu.VMEM(p.shape, BF) for p in parts] +
        [pltpu.VMEM((across, 4 * block, width), BF)] + [pltpu.VMEM((block, width), BF)] * 2 +
        [pltpu.VMEM(matrix.shape, BF), pltpu.SemaphoreType.DMA((max(len(parts), 1),)), pltpu.SemaphoreType.DMA((down,))],
        limit=12,
    )


def solution(mesh):
    in_specs = (P(None, "prow", None, "pcol"), P(), P(), P())
    out_specs = P(None, "prow", None, "pcol")
    return jax.shard_map(local, mesh=mesh, in_specs=in_specs, out_specs=out_specs, check_vma=False)
```
